768 devices in a mesh: sec: 48 (over x, z), dev: 16 (over y, core).
Axes of the slice: x: 4, y: 8, z: 12, core: 2. Of those that a mesh axis runs over, the one named last changes fastest.
Arguments:
- right_side: float32 [64, 98304], P(None, ('sec', 'dev')), may hold values from -6 to 6
- fine_blocks: bfloat16 [4, 64, 64, 98304], P(None, None, None, ('sec', 'dev'))
- fine_columns: int32 [3, 98304], P(None, ('sec', 'dev')), may hold values from 0 to 143
- send_rows: int32 [12288], P(('sec', 'dev')), may hold values from 0 to 127
- aggregate: int32 [98304], P(('sec', 'dev')), may hold values from 0 to 63
- coarse_blocks: bfloat16 [5, 64, 64, 3072], P(None, None, None, 'sec')
- coarse_columns: int32 [4, 3072], P(None, 'sec'), may hold values from 0 to 3071
- coarse_smoother: bfloat16 [64, 64, 3072], P(None, None, 'sec')
Outputs:
- solution: float32 [64, 98304], P(None, ('sec', 'dev'))
The draws below stay inside these ranges and needn't reach their ends.
Inputs may be any that keep to these rules, and one draw needn't show every extreme that they name: `fine_columns`: extended columns: below 8 come from the device below along dev, the next 128 are the device's own rows, the last 8 come from the device above. `send_rows`: each device's slots: the first 8 go to the device below along dev, the next 8 to the device above; indices are the device's own block rows, repeats allowed. `aggregate`: coarse row within the fine row's own section. `coarse_columns`: global coarse rows, of any section.
All inputs are finite; a program needn't handle non-finite values.
Results may differ from the reference program's by a relative error of at most 0.00035.
Values sent between devices are 32-bit elements; how exact they have to be, the bound alone decides.
A program may use at most 64 MiB of HBM per device.

```python
import math
import jax
import jax.numpy as jnp
from jax import lax

BLOCK = 64
ROWS_DEV = 128
HALO = 8
FINE_NNZ = 4
COARSE_NNZ = 5
COARSE_DEV = 4
CYCLES = 2
FINE_ROWS = 98304
SECTION_ROWS = 64
COARSE_ROWS = 3072
SEND_SLOTS = 12288
N_SEC = 48
N_DEV = 16


def noise_draw(key, shape):
    values = jax.random.normal(key, shape, jnp.float32)
    return jnp.clip(values, -3.0, 3.0)


def draw_fine_blocks(key, part):
    shape = (FINE_NNZ, BLOCK, BLOCK, FINE_ROWS)
    values = noise_draw(key, shape)
    slot = jnp.arange(FINE_NNZ)[:, None, None, None]
    level = jnp.where(slot == 0, 0.25, 0.3) / math.sqrt(BLOCK)
    eye = jnp.eye(BLOCK, dtype=jnp.float32)[None, :, :, None]
    return (jnp.where(slot == 0, 2.0, 0.0) * eye + level * values).astype(jnp.bfloat16)


def draw_coarse_blocks(key, part):
    shape = (COARSE_NNZ, BLOCK, BLOCK, COARSE_ROWS)
    values = noise_draw(key, shape)
    slot = jnp.arange(COARSE_NNZ)[:, None, None, None]
    level = jnp.where(slot == 0, 0.3, 0.4) / math.sqrt(BLOCK)
    eye = jnp.eye(BLOCK, dtype=jnp.float32)[None, :, :, None]
    return (jnp.where(slot == 0, 3.0, 0.0) * eye + level * values).astype(jnp.bfloat16)


def draw_coarse_smoother(key, part):
    values = noise_draw(key, (BLOCK, BLOCK, COARSE_ROWS))
    eye = jnp.eye(BLOCK, dtype=jnp.float32)[:, :, None]
    return (0.3 * eye + 0.04 / math.sqrt(BLOCK) * values).astype(jnp.bfloat16)


def plant(entries, stream_key, low, largest):
    dims = entries.shape
    index_at = [jax.random.randint(jax.random.fold_in(stream_key, axis), (), 0, dims[axis]) for axis in range(len(dims))]
    entries = entries.at[tuple(index_at)].set(low)
    longest = dims.index(max(dims))
    index_at[longest] = (index_at[longest] + 1) % dims[longest]
    return entries.at[tuple(index_at)].set(largest)


def steps_of(key, dims, cuts, smallest, largest):
    def one(axis_at, blocks):
        steps = jax.random.uniform(jax.random.fold_in(jax.random.fold_in(key, 6), axis_at), (blocks,), jnp.float32, smallest / len(cuts), largest / len(cuts))
        return jnp.repeat(jnp.exp(steps), dims[axis_at] // blocks).reshape((-1,) + (1,) * (len(dims) - axis_at - 1))

    gain = one(*cuts[0])
    for cut in cuts[1:]:
        gain = gain * one(*cut)
    return gain


def normal_values(rng, shape, deviation, reach, split=(), kind=jnp.bfloat16):
    entries = jax.random.normal(rng, shape, jnp.float32) * deviation
    if len(split) > 0:
        entries = steps_of(rng, shape, split, -0.22, 0.18) * entries
    return jnp.clip(entries, min=-reach, max=reach).astype(kind)


def setup_inputs(seed: int = 0) -> dict:
    splits = jax.random.split(jax.random.key(seed), 9)
    right_side = normal_values(splits[0], (BLOCK, FINE_ROWS), 1.0, 6.0, ((1, 768),), jnp.float32)
    fine_blocks = draw_fine_blocks(jax.random.fold_in(splits[8], 71), 0)
    fine_columns = plant(jax.random.randint(splits[2], (FINE_NNZ - 1, FINE_ROWS), 0, ROWS_DEV + 2 * HALO), jax.random.fold_in(splits[2], 1), 0, (ROWS_DEV + 2 * HALO) - 1).astype(jnp.int32)
    send_rows = plant(jax.random.randint(splits[3], (SEND_SLOTS,), 0, ROWS_DEV), jax.random.fold_in(splits[3], 1), 0, ROWS_DEV - 1).astype(jnp.int32)
    aggregate = plant(jax.random.randint(splits[4], (FINE_ROWS,), 0, SECTION_ROWS), jax.random.fold_in(splits[4], 1), 0, SECTION_ROWS - 1).astype(jnp.int32)
    coarse_blocks = draw_coarse_blocks(jax.random.fold_in(splits[8], 71), 0)
    coarse_columns = plant(jax.random.randint(splits[6], (COARSE_NNZ - 1, COARSE_ROWS), 0, COARSE_ROWS), jax.random.fold_in(splits[6], 1), 0, COARSE_ROWS - 1).astype(jnp.int32)
    coarse_smoother = draw_coarse_smoother(jax.random.fold_in(splits[8], 71), 0)
    return {"right_side": right_side, "fine_blocks": fine_blocks, "fine_columns": fine_columns, "send_rows": send_rows, "aggregate": aggregate, "coarse_blocks": coarse_blocks, "coarse_columns": coarse_columns, "coarse_smoother": coarse_smoother}


OMEGA = 0.45
PROLONG = 0.5
HIGH = lax.Precision.HIGHEST

def apply_section(state, blocks, columns, send_list):
    width = ROWS_DEV + 2 * HALO
    flat_state = state.reshape(BLOCK, N_DEV * ROWS_DEV)
    offsets = jnp.arange(N_DEV, dtype=jnp.int32)[:, None]
    outgoing = jnp.take(flat_state, (offsets * ROWS_DEV + send_list).astype(jnp.int32), axis=1)
    blank = jnp.zeros((BLOCK, 1, HALO), jnp.float32)
    lower = jnp.concatenate([blank, outgoing[:, :-1, HALO:]], axis=1)
    upper = jnp.concatenate([outgoing[:, 1:, :HALO], blank], axis=1)
    extended = jnp.concatenate([lower, state, upper], axis=2).reshape(BLOCK, N_DEV * width)
    picked = jnp.take(extended, (offsets[None] * width + columns).astype(jnp.int32), axis=1)
    own = jnp.einsum('ijtr,jtr->itr', blocks[0].astype(jnp.float32), state, precision=HIGH)
    near = jnp.einsum('kijtr,jktr->itr', blocks[1:].astype(jnp.float32), picked, precision=HIGH)
    return own + near

def reference(right_side, fine_blocks, fine_columns, send_rows, aggregate, coarse_blocks, coarse_columns, coarse_smoother):
    span = N_DEV * ROWS_DEV
    section_rows = COARSE_DEV * N_DEV
    weight = math.sqrt(COARSE_DEV / ROWS_DEV)
    pivots_all = jnp.diagonal(fine_blocks[0], axis1=0, axis2=1).astype(jnp.float32).T
    sections = jnp.arange(N_SEC, dtype=jnp.int32)

    def pieces(index):
        start = index * span
        rhs_part = lax.dynamic_slice_in_dim(right_side, start, span, 1).reshape(BLOCK, N_DEV, ROWS_DEV)
        block_part = lax.dynamic_slice_in_dim(fine_blocks, start, span, 3).reshape(FINE_NNZ, BLOCK, BLOCK, N_DEV, ROWS_DEV)
        column_part = lax.dynamic_slice_in_dim(fine_columns, start, span, 1).reshape(FINE_NNZ - 1, N_DEV, ROWS_DEV)
        send_part = lax.dynamic_slice_in_dim(send_rows, index * (N_DEV * 2 * HALO), N_DEV * 2 * HALO, 0).reshape(N_DEV, 2 * HALO)
        group_part = lax.dynamic_slice_in_dim(aggregate, start, span, 0).reshape(N_DEV, ROWS_DEV)
        pivot_part = lax.dynamic_slice_in_dim(pivots_all, start, span, 1).reshape(BLOCK, N_DEV, ROWS_DEV)
        return (rhs_part, block_part, column_part, send_part, group_part, pivot_part)

    def smooth(state, rhs_part, block_part, column_part, send_part, pivot_part):
        residual = rhs_part - apply_section(state, block_part, column_part, send_part)
        return state + OMEGA * residual / pivot_part

    def apply_coarse(vector):
        own = jnp.einsum('ijr,jr->ir', coarse_blocks[0].astype(jnp.float32), vector, precision=HIGH)
        picked = jnp.take(vector, coarse_columns, axis=1)
        near = jnp.einsum('kijr,jkr->ir', coarse_blocks[1:].astype(jnp.float32), picked, precision=HIGH)
        return own + near
    smoother_f = coarse_smoother.astype(jnp.float32)
    solution = jnp.zeros((BLOCK, N_SEC * span), jnp.float32)
    for repeat in range(CYCLES):

        def first_half(index):
            rhs_part, block_part, column_part, send_part, group_part, pivot_part = pieces(index)
            state = lax.dynamic_slice_in_dim(solution, index * span, span, 1).reshape(BLOCK, N_DEV, ROWS_DEV)
            state = smooth(state, rhs_part, block_part, column_part, send_part, pivot_part)
            residual = rhs_part - apply_section(state, block_part, column_part, send_part)
            onehot = (group_part.reshape(span)[:, None] == jnp.arange(section_rows, dtype=jnp.int32)[None, :]).astype(jnp.float32)
            partial_value = jnp.dot(residual.reshape(BLOCK, span), onehot, precision=HIGH)
            return (state.reshape(BLOCK, span), partial_value)
        states, partials = lax.map(first_half, sections)
        solution = jnp.transpose(states, (1, 0, 2)).reshape(BLOCK, N_SEC * span)
        coarse_rhs = jnp.transpose(partials, (1, 0, 2)).reshape(BLOCK, N_SEC * section_rows) * weight
        first = jnp.einsum('ijr,jr->ir', smoother_f, coarse_rhs, precision=HIGH)
        correction = first + jnp.einsum('ijr,jr->ir', smoother_f, coarse_rhs - apply_coarse(first), precision=HIGH)

        def second_half(index):
            rhs_part, block_part, column_part, send_part, group_part, pivot_part = pieces(index)
            state = lax.dynamic_slice_in_dim(solution, index * span, span, 1).reshape(BLOCK, N_DEV, ROWS_DEV)
            section_x = lax.dynamic_slice_in_dim(correction, index * section_rows, section_rows, 1)
            state = state + PROLONG * jnp.take(section_x, group_part, axis=1)
            state = smooth(state, rhs_part, block_part, column_part, send_part, pivot_part)
            return state.reshape(BLOCK, span)
        states = lax.map(second_half, sections)
        solution = jnp.transpose(states, (1, 0, 2)).reshape(BLOCK, N_SEC * span)
    return solution
```

```python
import functools
import math

import jax
import jax.numpy as jnp
from jax import lax
from jax.experimental import pallas as pl
from jax.experimental.pallas import tpu as pltpu
from jax.sharding import PartitionSpec as P

BLOCK = 64
ROWS = 128
HALO = 8
CYCLES = 2
N_DEV = 16
N_X = 4
N_Z = 12
N_SEC = N_X * N_Z
CHIPS = N_DEV // 2
COARSE = 64
SHARE = COARSE // CHIPS
OMEGA = 0.45
PROLONG = 0.5
MESH = pl.DeviceIdType.MESH
F32 = jnp.float32
BF16 = jnp.bfloat16
NT = (((1,), (1,)), ((), ()))
TN = (((0,), (0,)), ((), ()))
NN = (((1,), (0,)), ((), ()))


def pieces(value):
    high = value.astype(BF16)
    rest = value - high.astype(F32)
    middle = rest.astype(BF16)
    low = (rest - middle.astype(F32)).astype(BF16)
    return high, middle, low


def dot(a, b, dims):
    return lax.dot_general(a, b, dims, preferred_element_type=F32)


def select_right(value, onehot, dims):
    high, middle, low = pieces(value)
    return dot(high, onehot, dims) + dot(middle, onehot, dims) + dot(low, onehot, dims)


def select_left(onehot, value, dims):
    high, middle, low = pieces(value)
    return dot(onehot, high, dims) + dot(onehot, middle, dims) + dot(onehot, low, dims)


def iota(shape, axis):
    return lax.broadcasted_iota(jnp.int32, shape, axis)


def onehot_of(condition):
    return jnp.where(condition, 1.0, 0.0).astype(BF16)


def multiply(blocks, base, slots, tiles, x_ref, out_ref):
    lanes = x_ref.shape[-1]

    @pl.loop(0, tiles)
    def _(tile):
        row = tile * 8
        sums = [None] * 8
        for slot in range(slots):
            for part in range(BLOCK // 16):
                x = x_ref[slot, pl.ds(part * 16, 16), :]
                for a in range(8):
                    block = blocks(slot, base + row + a, part).astype(F32)
                    product = block * x
                    product = product[:8] + product[8:]
                    sums[a] = product if sums[a] is None else sums[a] + product
        index = iota((8, lanes), 0)
        total = jnp.zeros((8, lanes), F32)
        for a in range(8):
            total = jnp.where(index == a, jnp.sum(sums[a], axis=0, keepdims=True), total)
        out_ref[pl.ds(pl.multiple_of(row, 8), 8), :] = total


def kernel(
    weight,
    rhs_ref,
    fine_hbm,
    columns_ref,
    send_ref,
    aggregate_ref,
    coarse_hbm,
    ccolumns_ref,
    smoother_hbm,
    out_ref,
    fine,
    coarse,
    smoother,
    x_ref,
    ax_ref,
    pivots_ref,
    state_ref,
    pick_own,
    pick_halo,
    pick_section,
    pick_coarse,
    send_onehot,
    halo_out,
    halo_in,
    part_out,
    part_in,
    first_all,
    z_out,
    z_in,
    half_out,
    half_in,
    cx_ref,
    cy_ref,
    load_sem,
    send_sems,
    recv_sems,
):
    s = lax.axis_index("sec")
    t = lax.axis_index("dev")
    sx, sz = s // N_Z, lax.rem(s, N_Z)
    chip, core = t // 2, lax.rem(t, 2)

    def dev_peer(p):
        return (s, lax.rem(t + p, N_DEV))

    def sec_peer(p):
        dx, dz = p // N_Z, lax.rem(p, N_Z)
        return (lax.rem(sx + dx, N_X) * N_Z + lax.rem(sz + dz, N_Z), t)

    def chip_peer(p):
        return (s, lax.rem(t + 2 * p, N_DEV))

    other = (s, t + 1 - 2 * core)

    loads = [pltpu.make_async_copy(fine_hbm.at[k], fine.at[k], load_sem.at[k]) for k in range(4)]
    loads.append(pltpu.make_async_copy(smoother_hbm, smoother, load_sem.at[4]))
    loads.append(
        pltpu.make_async_copy(coarse_hbm.at[:, pl.ds(core * 32, 32)], coarse, load_sem.at[5])
    )
    for load in loads:
        load.start()

    barrier = pltpu.get_barrier_semaphore()

    @pl.loop(1, N_DEV)
    def _(p):
        pl.semaphore_signal(barrier, inc=1, device_id=dev_peer(p), device_id_type=MESH)

    @pl.loop(1, N_SEC)
    def _(p):
        pl.semaphore_signal(barrier, inc=1, device_id=sec_peer(p), device_id_type=MESH)

    aggregate = aggregate_ref[...]
    own_group = onehot_of(iota((COARSE, ROWS), 0) == aggregate)
    for k in range(3):
        column = columns_ref[pl.ds(k, 1), :]
        pick_own[:, pl.ds(k * ROWS, ROWS)] = onehot_of(iota((ROWS, ROWS), 0) == column - HALO)
        slot = iota((2 * HALO, ROWS), 0)
        where = jnp.where(slot < HALO, slot, slot + ROWS)
        pick_halo[:, pl.ds(k * ROWS, ROWS)] = onehot_of(where == column)
    send_onehot[...] = onehot_of(iota((2 * HALO, ROWS), 1) == send_ref[...])
    for k in range(4):
        column = ccolumns_ref[pl.ds(k, 1), :]
        section = column >> 6
        cx = (
            (section >= N_Z).astype(jnp.int32)
            + (section >= 2 * N_Z).astype(jnp.int32)
            + (section >= 3 * N_Z).astype(jnp.int32)
        )
        cz = section - cx * N_Z
        dx, dz = sx - cx, sz - cz
        dx = jnp.where(dx < 0, dx + N_X, dx)
        dz = jnp.where(dz < 0, dz + N_Z, dz)
        place = (dx * N_Z + dz) * SHARE + (column & (SHARE - 1))
        place = jnp.where(((column & (COARSE - 1)) >> 3) == chip, place, -1)
        pick_coarse[:, pl.ds(k * COARSE, COARSE)] = onehot_of(
            iota((N_SEC * SHARE, COARSE), 0) == place
        )
    own_rows = onehot_of(iota((SHARE, COARSE), 1) == chip * SHARE + iota((SHARE, COARSE), 0))

    loads[0].wait()
    index = iota((8, ROWS), 0)
    for tile in range(8):
        found = jnp.zeros((8, ROWS), F32)
        for a in range(8):
            i = tile * 8 + a
            near = fine[0, i, pl.ds(16 * (i // 16), 16), :].astype(F32)
            near = near[8 * (tile % 2) : 8 * (tile % 2) + 8]
            found = jnp.where(index == a, near, found)
        pivots_ref[pl.ds(tile * 8, 8), :] = found

    state_ref[...] = OMEGA * rhs_ref[...] / pivots_ref[...]

    def fine_block(slot, i, part):
        return fine[slot, i, pl.ds(part * 16, 16), :]

    def coarse_block(slot, i, part):
        return coarse[slot, i, pl.ds(part * 16, 16), :]

    def smoother_block(slot, i, part):
        return smoother[i, pl.ds(part * 16, 16), :]

    def wait_for(ref, sem):
        pltpu.make_async_copy(ref, ref, sem).wait()

    def halo_exchange(turn, with_groups):
        high, middle, low = pieces(state_ref[...])
        picked = (
            dot(send_onehot[...], high, NT)
            + dot(send_onehot[...], middle, NT)
            + dot(send_onehot[...], low, NT)
        )
        if with_groups:
            groups = dot(send_onehot[...], own_group, NT)
        else:
            groups = jnp.zeros((2 * HALO, COARSE), F32)
        halo_out[turn] = jnp.concatenate([picked, groups], axis=1)
        if turn == 0:
            pl.semaphore_wait(barrier, N_DEV - 1 + N_SEC - 1)
        down = pltpu.make_async_remote_copy(
            src_ref=halo_out.at[turn, pl.ds(0, HALO)],
            dst_ref=halo_in.at[turn, pl.ds(HALO, HALO)],
            send_sem=send_sems.at[turn, 0],
            recv_sem=recv_sems.at[turn, 0],
            device_id=dev_peer(N_DEV - 1),
            device_id_type=MESH,
        )
        up = pltpu.make_async_remote_copy(
            src_ref=halo_out.at[turn, pl.ds(HALO, HALO)],
            dst_ref=halo_in.at[turn, pl.ds(0, HALO)],
            send_sem=send_sems.at[turn, 1],
            recv_sem=recv_sems.at[turn, 1],
            device_id=dev_peer(1),
            device_id_type=MESH,
        )
        down.start()
        up.start()
        x_ref[0] = state_ref[...]
        own = (
            dot(high, pick_own[...], NN) + dot(middle, pick_own[...], NN) + dot(low, pick_own[...], NN)
        )
        down.wait()
        up.wait()
        slot = iota((2 * HALO, ROWS), 0)
        there = ((slot < HALO) & (t > 0)) | ((slot >= HALO) & (t < N_DEV - 1))
        halo = jnp.where(there, halo_in[turn], 0.0)
        picked = own + select_right(halo[:, :BLOCK], pick_halo[...], TN)
        for k in range(3):
            x_ref[k + 1] = picked[:, k * ROWS : (k + 1) * ROWS]
        if with_groups:
            pick_section[:, pl.ds(0, ROWS)] = own_group
            pick_section[:, pl.ds(ROWS, 3 * ROWS)] = (
                dot(own_group, pick_own[...], NN)
                + dot(halo[:, BLOCK:].astype(BF16), pick_halo[...], TN)
            ).astype(BF16)

    for cycle in range(CYCLES):
        base = 4 * cycle + 3
        if cycle > 0:
            halo_exchange(1, False)
            multiply(fine_block, 0, 4, 8, x_ref, ax_ref)
            state_ref[...] += OMEGA * (rhs_ref[...] - ax_ref[...]) / pivots_ref[...]
        halo_exchange(2 * cycle, cycle == 0)
        if cycle == 0:
            for load in loads[1:4]:
                load.wait()
        multiply(fine_block, 0, 4, 8, x_ref, ax_ref)
        residual = rhs_ref[...] - ax_ref[...]
        part_out[cycle] = (select_left(own_group, residual, NT) * weight).reshape(
            CHIPS, SHARE, BLOCK
        )

        @pl.loop(1, N_DEV)
        def _(p):
            pltpu.make_async_remote_copy(
                src_ref=part_out.at[cycle, lax.rem(t + p, N_DEV) // 2],
                dst_ref=part_in.at[cycle, p - 1],
                send_sem=send_sems.at[base, 0],
                recv_sem=recv_sems.at[base, 0],
                device_id=dev_peer(p),
                device_id_type=MESH,
            ).start()

        if cycle == 0:
            for load in loads[4:]:
                load.wait()
        wait_for(part_in.at[cycle], recv_sems.at[base, 0])
        rhs_rows = part_out[cycle, chip] + jnp.sum(part_in[cycle], axis=0)
        coarse_rhs = select_right(rhs_rows, own_rows, TN)
        cx_ref[0] = coarse_rhs
        multiply(smoother_block, 0, 1, 8, cx_ref, cy_ref)
        first = cy_ref[...]
        first_all[cycle, 0] = select_left(own_rows, first, NT)

        @pl.loop(1, N_SEC)
        def _(p):
            pltpu.make_async_remote_copy(
                src_ref=first_all.at[cycle, 0],
                dst_ref=first_all.at[cycle, p],
                send_sem=send_sems.at[base + 1, 0],
                recv_sem=recv_sems.at[base + 1, 0],
                device_id=sec_peer(p),
                device_id_type=MESH,
            ).start()

        cx_ref[0] = first
        wait_for(first_all.at[cycle, pl.ds(1, N_SEC - 1)], recv_sems.at[base + 1, 0])
        held = first_all[cycle].reshape(N_SEC * SHARE, BLOCK)
        picked = select_right(held, pick_coarse[...], TN)
        for k in range(4):
            cx_ref[k + 1] = picked[:, k * COARSE : (k + 1) * COARSE]
        multiply(coarse_block, 0, 5, 4, cx_ref, cy_ref)
        own_half = jnp.where(core == 0, coarse_rhs[:32], coarse_rhs[32:])
        z = 2.0 * own_half - cy_ref[pl.ds(0, 32), :]
        z_out[cycle] = jnp.concatenate([z[:16], z[16:]], axis=1)

        @pl.loop(1, CHIPS)
        def _(p):
            pltpu.make_async_remote_copy(
                src_ref=z_out.at[cycle],
                dst_ref=z_in.at[cycle, p - 1],
                send_sem=send_sems.at[base + 2, 0],
                recv_sem=recv_sems.at[base + 2, 0],
                device_id=chip_peer(p),
                device_id_type=MESH,
            ).start()

        wait_for(z_in.at[cycle], recv_sems.at[base + 2, 0])
        half_out[cycle] = z_out[cycle] + jnp.sum(z_in[cycle], axis=0)
        pair = pltpu.make_async_remote_copy(
            src_ref=half_out.at[cycle],
            dst_ref=half_in.at[cycle],
            send_sem=send_sems.at[base + 3, 0],
            recv_sem=recv_sems.at[base + 3, 0],
            device_id=other,
            device_id_type=MESH,
        )
        pair.start()
        pair.wait()
        mine, theirs = half_out[cycle], half_in[cycle]
        lower = jnp.where(core == 0, mine, theirs)
        upper = jnp.where(core == 0, theirs, mine)
        cx_ref[0] = jnp.concatenate(
            [lower[:, :COARSE], lower[:, COARSE:], upper[:, :COARSE], upper[:, COARSE:]], axis=0
        )
        multiply(smoother_block, 0, 1, 8, cx_ref, cy_ref)
        picked = select_right(cy_ref[...], pick_section[...], NN)
        for k in range(4):
            x_ref[k] = picked[:, k * ROWS : (k + 1) * ROWS]
        multiply(fine_block, 0, 4, 8, x_ref, ax_ref)
        state_ref[...] += PROLONG * x_ref[0] + OMEGA * (residual - PROLONG * ax_ref[...]) / (
            pivots_ref[...]
        )

        wait_for(part_in.at[cycle], send_sems.at[base, 0])
        wait_for(first_all.at[cycle, pl.ds(1, N_SEC - 1)], send_sems.at[base + 1, 0])
        wait_for(z_in.at[cycle], send_sems.at[base + 2, 0])

    out_ref[...] = state_ref[...]


def shards(
    right_side,
    fine_blocks,
    fine_columns,
    send_rows,
    aggregate,
    coarse_blocks,
    coarse_columns,
    coarse_smoother,
):
    vmem = pl.BlockSpec(memory_space=pltpu.VMEM)
    hbm = pl.BlockSpec(memory_space=pl.ANY)
    phases = 3 + 4 * CYCLES
    return pl.pallas_call(
        functools.partial(kernel, math.sqrt(4 / ROWS)),
        out_shape=jax.ShapeDtypeStruct((BLOCK, ROWS), F32),
        in_specs=[vmem, hbm, vmem, vmem, vmem, hbm, vmem, hbm],
        out_specs=vmem,
        scratch_shapes=[
            pltpu.VMEM((4, BLOCK, BLOCK, ROWS), BF16),
            pltpu.VMEM((5, BLOCK // 2, BLOCK, COARSE), BF16),
            pltpu.VMEM((BLOCK, BLOCK, COARSE), BF16),
            pltpu.VMEM((4, BLOCK, ROWS), F32),
            pltpu.VMEM((BLOCK, ROWS), F32),
            pltpu.VMEM((BLOCK, ROWS), F32),
            pltpu.VMEM((BLOCK, ROWS), F32),
            pltpu.VMEM((ROWS, 3 * ROWS), BF16),
            pltpu.VMEM((2 * HALO, 3 * ROWS), BF16),
            pltpu.VMEM((COARSE, 4 * ROWS), BF16),
            pltpu.VMEM((N_SEC * SHARE, 4 * COARSE), BF16),
            pltpu.VMEM((2 * HALO, ROWS), BF16),
            pltpu.VMEM((3, 2 * HALO, 2 * BLOCK), F32),
            pltpu.VMEM((3, 2 * HALO, 2 * BLOCK), F32),
            pltpu.VMEM((CYCLES, CHIPS, SHARE, BLOCK), F32),
            pltpu.VMEM((CYCLES, N_DEV - 1, SHARE, BLOCK), F32),
            pltpu.VMEM((CYCLES, N_SEC, SHARE, BLOCK), F32),
            pltpu.VMEM((CYCLES, 16, 2 * COARSE), F32),
            pltpu.VMEM((CYCLES, CHIPS - 1, 16, 2 * COARSE), F32),
            pltpu.VMEM((CYCLES, 16, 2 * COARSE), F32),
            pltpu.VMEM((CYCLES, 16, 2 * COARSE), F32),
            pltpu.VMEM((5, BLOCK, COARSE), F32),
            pltpu.VMEM((BLOCK, COARSE), F32),
            pltpu.SemaphoreType.DMA((6,)),
            pltpu.SemaphoreType.DMA((phases, 2)),
            pltpu.SemaphoreType.DMA((phases, 2)),
        ],
        compiler_params=pltpu.CompilerParams(
            collective_id=0, has_side_effects=True, vmem_limit_bytes=48 * 1024 * 1024
        ),
        name="cycles",
    )(
        right_side,
        fine_blocks,
        fine_columns,
        send_rows.reshape(2 * HALO, 1),
        aggregate.reshape(1, ROWS),
        coarse_blocks,
        coarse_columns,
        coarse_smoother,
    )


def solution(mesh):
    placed = (
        P(None, ("sec", "dev")),
        P(None, None, None, ("sec", "dev")),
        P(None, ("sec", "dev")),
        P(("sec", "dev")),
        P(("sec", "dev")),
        P(None, None, None, "sec"),
        P(None, "sec"),
        P(None, None, "sec"),
    )
    return jax.shard_map(
        shards, mesh=mesh, in_specs=placed, out_specs=P(None, ("sec", "dev")), check_vma=False
    )
```

```python
import functools
import math

import jax
import jax.numpy as jnp
from jax import lax
from jax.experimental import pallas as pl
from jax.experimental.pallas import tpu as pltpu
from jax.sharding import PartitionSpec as P

BLOCK = 64
ROWS = 128
HALO = 8
CYCLES = 2
N_DEV = 16
N_X = 4
N_Z = 12
N_SEC = N_X * N_Z
CHIPS = N_DEV // 2
COARSE = 64
OMEGA = 0.45
PROLONG = 0.5
MESH = pl.DeviceIdType.MESH
F32 = jnp.float32
BF16 = jnp.bfloat16
NT = (((1,), (1,)), ((), ()))
TN = (((0,), (0,)), ((), ()))
NN = (((1,), (0,)), ((), ()))


def ring(step, count):
    return min(step, count - step)


SEC_ORDER = sorted(
    range(1, N_SEC), key=lambda p: -(ring(p // N_Z, N_X) + ring(p % N_Z, N_Z))
)
DEV_ORDER = sorted(range(1, N_DEV), key=lambda p: -ring(p, N_DEV))
CHIP_ORDER = sorted(range(1, CHIPS), key=lambda p: -ring(p, CHIPS))


def pieces(value):
    high = value.astype(BF16)
    rest = value - high.astype(F32)
    middle = rest.astype(BF16)
    low = (rest - middle.astype(F32)).astype(BF16)
    return high, middle, low


def dot(a, b, dims):
    return lax.dot_general(a, b, dims, preferred_element_type=F32)


def select_right(value, onehot, dims):
    high, middle, low = pieces(value)
    return dot(high, onehot, dims) + dot(middle, onehot, dims) + dot(low, onehot, dims)


def select_left(onehot, value, dims):
    high, middle, low = pieces(value)
    return dot(onehot, high, dims) + dot(onehot, middle, dims) + dot(onehot, low, dims)


def iota(shape, axis):
    return lax.broadcasted_iota(jnp.int32, shape, axis)


def onehot_of(condition):
    return jnp.where(condition, 1.0, 0.0).astype(BF16)


def twice(value):
    return jnp.concatenate([value, value], axis=1)


def unpaired(value):
    return jnp.concatenate([value[:, :COARSE], value[:, COARSE:]], axis=0)


def multiply(blocks, slots, tiles, x_ref, out_ref, add=False):
    lanes = x_ref.shape[-1]

    @pl.loop(0, tiles)
    def _(tile):
        row = tile * 8
        sums = [None] * 8
        for slot in slots:
            for part in range(BLOCK // 16):
                x = x_ref[slot, pl.ds(part * 16, 16), :]
                for a in range(8):
                    block = blocks(slot, row + a, part).astype(F32)
                    product = block * x
                    product = product[:8] + product[8:]
                    sums[a] = product if sums[a] is None else sums[a] + product
        index = iota((8, lanes), 0)
        total = jnp.zeros((8, lanes), F32)
        for a in range(8):
            total = jnp.where(index == a, jnp.sum(sums[a], axis=0, keepdims=True), total)
        place = pl.ds(pl.multiple_of(row, 8), 8)
        out_ref[place, :] = out_ref[place, :] + total if add else total


def kernel(
    weight,
    rhs_hbm,
    fine_hbm,
    columns_hbm,
    send_hbm,
    aggregate_hbm,
    coarse_hbm,
    ccolumns_hbm,
    smoother_hbm,
    out_ref,
    rhs_ref,
    columns_ref,
    send_ref,
    aggregate_ref,
    ccolumns_ref,
    fine,
    coarse,
    smoother,
    coarse_raw,
    smoother_raw,
    x_ref,
    ax_ref,
    pivots_ref,
    state_ref,
    pick_own,
    pick_halo,
    pick_section,
    pick_coarse,
    send_onehot,
    halo_out,
    halo_in,
    part_out,
    part_in,
    first_all,
    z_out,
    z_in,
    half_out,
    half_in,
    cx_ref,
    cy_ref,
    load_sem,
    send_sems,
    recv_sems,
):
    s = lax.axis_index("sec")
    t = lax.axis_index("dev")
    sx, sz = s // N_Z, lax.rem(s, N_Z)
    chip, core = t // 2, lax.rem(t, 2)

    def dev_peer(p):
        return (s, (t + p) & (N_DEV - 1))

    def sec_peer(p):
        dx, dz = p // N_Z, p % N_Z
        z = sz + dz
        z = jnp.where(z >= N_Z, z - N_Z, z)
        return (((sx + dx) & (N_X - 1)) * N_Z + z, t)

    def chip_peer(p):
        return (s, (t + 2 * p) & (N_DEV - 1))

    other = (s, t + 1 - 2 * core)

    barrier = pltpu.get_barrier_semaphore()

    for p in SEC_ORDER:
        pl.semaphore_signal(barrier, inc=1, device_id=sec_peer(p), device_id_type=MESH)
    for p in DEV_ORDER:
        pl.semaphore_signal(barrier, inc=1, device_id=dev_peer(p), device_id_type=MESH)

    loads = [pltpu.make_async_copy(fine_hbm.at[k], fine.at[k], load_sem.at[k]) for k in range(4)]
    small = [
        pltpu.make_async_copy(*pair, load_sem.at[6 + n])
        for n, pair in enumerate(
            (
                (rhs_hbm, rhs_ref),
                (columns_hbm, columns_ref),
                (send_hbm, send_ref),
                (aggregate_hbm, aggregate_ref),
                (ccolumns_hbm, ccolumns_ref),
            )
        )
    ]
    for load in small:
        load.start()
    loads.append(pltpu.make_async_copy(smoother_hbm, smoother_raw, load_sem.at[4]))
    loads.append(
        pltpu.make_async_copy(coarse_hbm.at[:, pl.ds(core * 32, 32)], coarse_raw, load_sem.at[5])
    )
    for load in loads:
        load.start()
    for load in small:
        load.wait()

    aggregate = aggregate_ref[...]
    own_group = onehot_of(iota((COARSE, ROWS), 0) == aggregate)
    sent = jnp.concatenate(
        [send_ref[...], jnp.full((1, ROWS - 2 * HALO), -1, jnp.int32)], axis=1
    )
    sent = jnp.where(iota((ROWS, ROWS), 0) == sent, 1.0, 0.0).T
    send_onehot[...] = sent[: 2 * HALO].astype(BF16)
    row = iota((16, COARSE), 0)
    own_low = onehot_of((iota((16, COARSE), 1) == chip * 4 + row) & (row < 4))
    own_high = onehot_of((iota((16, COARSE), 1) == chip * 4 + 32 + row) & (row < 4))

    def fine_tables():
        for k in range(3):
            column = columns_ref[pl.ds(k, 1), :]
            pick_own[:, pl.ds(k * ROWS, ROWS)] = onehot_of(iota((ROWS, ROWS), 0) == column - HALO)
            slot = iota((2 * HALO, ROWS), 0)
            where = jnp.where(slot < HALO, slot, slot + ROWS)
            pick_halo[:, pl.ds(k * ROWS, ROWS)] = onehot_of(where == column)

    def coarse_tables():
        for k in range(4):
            column = ccolumns_ref[pl.ds(k, 1), :]
            section = column >> 6
            cx = (
                (section >= N_Z).astype(jnp.int32)
                + (section >= 2 * N_Z).astype(jnp.int32)
                + (section >= 3 * N_Z).astype(jnp.int32)
            )
            cz = section - cx * N_Z
            dx, dz = sx - cx, sz - cz
            dx = jnp.where(dx < 0, dx + N_X, dx)
            dz = jnp.where(dz < 0, dz + N_Z, dz)
            place = (dx * N_Z + dz) * 4 + (column & 3)
            place = jnp.where(((column & 31) >> 2) == chip, place, -1)
            for half in range(2):
                here = jnp.where(((column >> 5) & 1) == half, place, -1)
                pick_coarse[:, pl.ds((4 * half + k) * COARSE, COARSE)] = onehot_of(
                    iota((N_SEC * 4, COARSE), 0) == here
                )

    loads[0].wait()
    index = iota((8, ROWS), 0)
    for tile in range(8):
        found = jnp.zeros((8, ROWS), F32)
        for a in range(8):
            i = tile * 8 + a
            near = fine[0, i, pl.ds(16 * (i // 16), 16), :].astype(F32)
            near = near[8 * (tile % 2) : 8 * (tile % 2) + 8]
            found = jnp.where(index == a, near, found)
        pivots_ref[pl.ds(tile * 8, 8), :] = found

    state_ref[...] = OMEGA * rhs_ref[...] / pivots_ref[...]

    def fine_block(slot, i, part):
        return fine[slot, i, pl.ds(part * 16, 16), :]

    def coarse_block(slot, i, part):
        return coarse[slot, i, pl.ds(part * 16, 16), :]

    def smoother_block(slot, i, part):
        return smoother[i, pl.ds(part * 16, 16), :]

    def wait_for(ref, sem):
        pltpu.make_async_copy(ref, ref, sem).wait()

    def halo_exchange(turn, with_groups):
        high, middle, low = pieces(state_ref[...])
        picked = (
            dot(send_onehot[...], high, NT)
            + dot(send_onehot[...], middle, NT)
            + dot(send_onehot[...], low, NT)
        )
        if with_groups:
            groups = dot(send_onehot[...], own_group, NT)
        else:
            groups = jnp.zeros((2 * HALO, COARSE), F32)
        halo_out[turn] = jnp.concatenate([picked, groups], axis=1)
        if turn == 0:
            pl.semaphore_wait(barrier, N_DEV - 1 + N_SEC - 1)
        down = pltpu.make_async_remote_copy(
            src_ref=halo_out.at[turn, pl.ds(0, HALO)],
            dst_ref=halo_in.at[turn, pl.ds(HALO, HALO)],
            send_sem=send_sems.at[turn, 0],
            recv_sem=recv_sems.at[turn, 0],
            device_id=dev_peer(N_DEV - 1),
            device_id_type=MESH,
        )
        up = pltpu.make_async_remote_copy(
            src_ref=halo_out.at[turn, pl.ds(HALO, HALO)],
            dst_ref=halo_in.at[turn, pl.ds(0, HALO)],
            send_sem=send_sems.at[turn, 1],
            recv_sem=recv_sems.at[turn, 1],
            device_id=dev_peer(1),
            device_id_type=MESH,
        )
        down.start()
        up.start()
        x_ref[0] = state_ref[...]
        if turn == 0:
            fine_tables()
        multiply(fine_block, (0,), 8, x_ref, ax_ref)
        own = (
            dot(high, pick_own[...], NN) + dot(middle, pick_own[...], NN) + dot(low, pick_own[...], NN)
        )
        down.wait_recv()
        up.wait_recv()
        slot = iota((2 * HALO, ROWS), 0)
        there = ((slot < HALO) & (t > 0)) | ((slot >= HALO) & (t < N_DEV - 1))
        halo = jnp.where(there, halo_in[turn], 0.0)
        picked = own + select_right(halo[:, :BLOCK], pick_halo[...], TN)
        for k in range(3):
            x_ref[k + 1] = picked[:, k * ROWS : (k + 1) * ROWS]
        if with_groups:
            pick_section[:, pl.ds(0, ROWS)] = own_group
            pick_section[:, pl.ds(ROWS, 3 * ROWS)] = (
                dot(own_group, pick_own[...], NN)
                + dot(halo[:, BLOCK:].astype(BF16), pick_halo[...], TN)
            ).astype(BF16)
            for load in loads[1:4]:
                load.wait()
        multiply(fine_block, (1, 2, 3), 8, x_ref, ax_ref, add=True)
        return down, up

    halo_copies = ()
    for cycle in range(CYCLES):
        base = 4 * cycle + 3
        if cycle > 0:
            halo_copies += halo_exchange(1, False)
            state_ref[...] += OMEGA * (rhs_ref[...] - ax_ref[...]) / pivots_ref[...]
        halo_copies += halo_exchange(2 * cycle, cycle == 0)
        residual = rhs_ref[...] - ax_ref[...]
        partial = select_left(own_group, residual, NT) * weight
        part_out[cycle] = jnp.concatenate([partial[:32], partial[32:]], axis=1).reshape(
            CHIPS, 4, 2 * BLOCK
        )

        for p in DEV_ORDER:
            pltpu.make_async_remote_copy(
                src_ref=part_out.at[cycle, ((t + p) & (N_DEV - 1)) >> 1],
                dst_ref=part_in.at[cycle, p - 1],
                send_sem=send_sems.at[base, 0],
                recv_sem=recv_sems.at[base, 0],
                device_id=dev_peer(p),
                device_id_type=MESH,
            ).start()

        if cycle == 0:
            loads[4].wait()

            @pl.loop(0, 32)
            def _(i):
                smoother[i] = jnp.concatenate([smoother_raw[i], smoother_raw[i + 32]], axis=1)

            coarse_tables()
        wait_for(part_in.at[cycle], recv_sems.at[base, 0])
        rhs_rows = part_out[cycle, chip] + jnp.sum(part_in[cycle], axis=0)
        rhs_rows = jnp.concatenate([rhs_rows, jnp.zeros((12, 2 * BLOCK), F32)], axis=0)
        coarse_rhs = select_right(rhs_rows[:, :BLOCK], own_low, TN) + select_right(
            rhs_rows[:, BLOCK:], own_high, TN
        )
        cx_ref[0] = twice(coarse_rhs)
        multiply(smoother_block, (0,), 4, cx_ref, cy_ref)
        first = unpaired(cy_ref[...])
        first_all[cycle, 0] = jnp.concatenate(
            [select_left(own_low, first, NT)[:4], select_left(own_high, first, NT)[:4]], axis=1
        )

        for p in SEC_ORDER:
            pltpu.make_async_remote_copy(
                src_ref=first_all.at[cycle, 0],
                dst_ref=first_all.at[cycle, p],
                send_sem=send_sems.at[base + 1, 0],
                recv_sem=recv_sems.at[base + 1, 0],
                device_id=sec_peer(p),
                device_id_type=MESH,
            ).start()

        if cycle == 0:
            loads[5].wait()

            @pl.loop(0, 16)
            def _(i):
                for k in range(5):
                    coarse[k, i] = jnp.concatenate([coarse_raw[k, i], coarse_raw[k, i + 16]], axis=1)

        cx_ref[0] = twice(first)
        multiply(coarse_block, (0,), 2, cx_ref, cy_ref)
        wait_for(first_all.at[cycle, pl.ds(1, N_SEC - 1)], recv_sems.at[base + 1, 0])
        held = first_all[cycle].reshape(N_SEC * 4, 2 * BLOCK)
        picked = select_right(held, pick_coarse[...], TN)
        picked = picked[:BLOCK, : 4 * COARSE] + picked[BLOCK:, 4 * COARSE :]
        for k in range(4):
            cx_ref[k + 1] = twice(picked[:, k * COARSE : (k + 1) * COARSE])
        multiply(coarse_block, (1, 2, 3, 4), 2, cx_ref, cy_ref, add=True)
        own_half = jnp.where(core == 0, coarse_rhs[:32], coarse_rhs[32:])
        own_half = jnp.concatenate([own_half[:16], own_half[16:]], axis=1)
        z_out[cycle] = 2.0 * own_half - cy_ref[pl.ds(0, 16), :]

        for p in CHIP_ORDER:
            pltpu.make_async_remote_copy(
                src_ref=z_out.at[cycle],
                dst_ref=z_in.at[cycle, p - 1],
                send_sem=send_sems.at[base + 2, 0],
                recv_sem=recv_sems.at[base + 2, 0],
                device_id=chip_peer(p),
                device_id_type=MESH,
            ).start()

        wait_for(z_in.at[cycle], recv_sems.at[base + 2, 0])
        half_out[cycle] = z_out[cycle] + jnp.sum(z_in[cycle], axis=0)
        pair = pltpu.make_async_remote_copy(
            src_ref=half_out.at[cycle],
            dst_ref=half_in.at[cycle],
            send_sem=send_sems.at[base + 3, 0],
            recv_sem=recv_sems.at[base + 3, 0],
            device_id=other,
            device_id_type=MESH,
        )
        pair.start()
        pair.wait_recv()
        mine, theirs = half_out[cycle], half_in[cycle]
        lower = jnp.where(core == 0, mine, theirs)
        upper = jnp.where(core == 0, theirs, mine)
        cx_ref[0] = twice(jnp.concatenate([unpaired(lower), unpaired(upper)], axis=0))
        multiply(smoother_block, (0,), 4, cx_ref, cy_ref)
        picked = select_right(unpaired(cy_ref[...]), pick_section[...], NN)
        for k in range(4):
            x_ref[k] = picked[:, k * ROWS : (k + 1) * ROWS]
        multiply(fine_block, (0, 1, 2, 3), 8, x_ref, ax_ref)
        state_ref[...] += PROLONG * x_ref[0] + OMEGA * (residual - PROLONG * ax_ref[...]) / (
            pivots_ref[...]
        )

        wait_for(part_in.at[cycle], send_sems.at[base, 0])
        wait_for(first_all.at[cycle, pl.ds(1, N_SEC - 1)], send_sems.at[base + 1, 0])
        wait_for(z_in.at[cycle], send_sems.at[base + 2, 0])
        pair.wait_send()

    out_ref[...] = state_ref[...]
    for copy in halo_copies:
        copy.wait_send()


def shards(
    right_side,
    fine_blocks,
    fine_columns,
    send_rows,
    aggregate,
    coarse_blocks,
    coarse_columns,
    coarse_smoother,
):
    vmem = pl.BlockSpec(memory_space=pltpu.VMEM)
    hbm = pl.BlockSpec(memory_space=pl.ANY)
    phases = 3 + 4 * CYCLES
    return pl.pallas_call(
        functools.partial(kernel, math.sqrt(4 / ROWS)),
        out_shape=jax.ShapeDtypeStruct((BLOCK, ROWS), F32),
        in_specs=[hbm] * 8,
        out_specs=vmem,
        scratch_shapes=[
            pltpu.VMEM((BLOCK, ROWS), F32),
            pltpu.VMEM((3, ROWS), jnp.int32),
            pltpu.VMEM((1, 2 * HALO), jnp.int32),
            pltpu.VMEM((1, ROWS), jnp.int32),
            pltpu.VMEM((4, COARSE), jnp.int32),
            pltpu.VMEM((4, BLOCK, BLOCK, ROWS), BF16),
            pltpu.VMEM((5, BLOCK // 4, BLOCK, 2 * COARSE), BF16),
            pltpu.VMEM((BLOCK // 2, BLOCK, 2 * COARSE), BF16),
            pltpu.VMEM((5, BLOCK // 2, BLOCK, COARSE), BF16),
            pltpu.VMEM((BLOCK, BLOCK, COARSE), BF16),
            pltpu.VMEM((4, BLOCK, ROWS), F32),
            pltpu.VMEM((BLOCK, ROWS), F32),
            pltpu.VMEM((BLOCK, ROWS), F32),
            pltpu.VMEM((BLOCK, ROWS), F32),
            pltpu.VMEM((ROWS, 3 * ROWS), BF16),
            pltpu.VMEM((2 * HALO, 3 * ROWS), BF16),
            pltpu.VMEM((COARSE, 4 * ROWS), BF16),
            pltpu.VMEM((N_SEC * 4, 8 * COARSE), BF16),
            pltpu.VMEM((2 * HALO, ROWS), BF16),
            pltpu.VMEM((3, 2 * HALO, 2 * BLOCK), F32),
            pltpu.VMEM((3, 2 * HALO, 2 * BLOCK), F32),
            pltpu.VMEM((CYCLES, CHIPS, 4, 2 * BLOCK), F32),
            pltpu.VMEM((CYCLES, N_DEV - 1, 4, 2 * BLOCK), F32),
            pltpu.VMEM((CYCLES, N_SEC, 4, 2 * BLOCK), F32),
            pltpu.VMEM((CYCLES, 16, 2 * COARSE), F32),
            pltpu.VMEM((CYCLES, CHIPS - 1, 16, 2 * COARSE), F32),
            pltpu.VMEM((CYCLES, 16, 2 * COARSE), F32),
            pltpu.VMEM((CYCLES, 16, 2 * COARSE), F32),
            pltpu.VMEM((5, BLOCK, 2 * COARSE), F32),
            pltpu.VMEM((BLOCK // 2, 2 * COARSE), F32),
            pltpu.SemaphoreType.DMA((11,)),
            pltpu.SemaphoreType.DMA((phases, 2)),
            pltpu.SemaphoreType.DMA((phases, 2)),
        ],
        compiler_params=pltpu.CompilerParams(
            collective_id=0, has_side_effects=True, vmem_limit_bytes=60 * 1024 * 1024
        ),
        name="cycles",
    )(
        right_side,
        fine_blocks,
        fine_columns,
        send_rows.reshape(1, 2 * HALO),
        aggregate.reshape(1, ROWS),
        coarse_blocks,
        coarse_columns,
        coarse_smoother,
    )


def solution(mesh):
    placed = (
        P(None, ("sec", "dev")),
        P(None, None, None, ("sec", "dev")),
        P(None, ("sec", "dev")),
        P(("sec", "dev")),
        P(("sec", "dev")),
        P(None, None, None, "sec"),
        P(None, "sec"),
        P(None, None, "sec"),
    )
    return jax.shard_map(
        shards, mesh=mesh, in_specs=placed, out_specs=P(None, ("sec", "dev")), check_vma=False
    )
```

```python
import functools
import math

import jax
import jax.numpy as jnp
from jax import lax
from jax.experimental import pallas as pl
from jax.experimental.pallas import tpu as pltpu
from jax.sharding import PartitionSpec as P

BLOCK = 64
ROWS = 128
HALO = 8
CYCLES = 2
N_DEV = 16
N_X = 4
N_Z = 12
N_SEC = N_X * N_Z
CHIPS = N_DEV // 2
COARSE = 64
OMEGA = 0.45
PROLONG = 0.5
MESH = pl.DeviceIdType.MESH
F32 = jnp.float32
BF16 = jnp.bfloat16
NT = (((1,), (1,)), ((), ()))
TN = (((0,), (0,)), ((), ()))
NN = (((1,), (0,)), ((), ()))


def ring(step, count):
    return min(step, count - step)


SEC_ORDER = sorted(
    range(1, N_SEC), key=lambda p: -(ring(p // N_Z, N_X) + ring(p % N_Z, N_Z))
)
DEV_ORDER = sorted(range(1, N_DEV), key=lambda p: -ring(p, N_DEV))
CHIP_ORDER = sorted(range(1, CHIPS), key=lambda p: -ring(p, CHIPS))


def pieces(value):
    high = value.astype(BF16)
    low = (value - high.astype(F32)).astype(BF16)
    return high, low


def dot(a, b, dims):
    return lax.dot_general(a, b, dims, preferred_element_type=F32)


def select_right(value, onehot, dims):
    high, low = pieces(value)
    return dot(high, onehot, dims) + dot(low, onehot, dims)


def select_left(onehot, value, dims):
    high, low = pieces(value)
    return dot(onehot, high, dims) + dot(onehot, low, dims)


def iota(shape, axis):
    return lax.broadcasted_iota(jnp.int32, shape, axis)


def onehot_of(condition):
    return jnp.where(condition, 1.0, 0.0).astype(BF16)


def twice(value):
    return jnp.concatenate([value, value], axis=1)


def unpaired(value):
    return jnp.concatenate([value[:, :COARSE], value[:, COARSE:]], axis=0)


def multiply(blocks, slots, tiles, x_ref, out_ref, add=False):
    lanes = x_ref.shape[-1]

    @pl.loop(0, tiles)
    def _(tile):
        row = tile * 8
        sums = [None] * 8
        for slot in slots:
            for part in range(BLOCK // 16):
                x = x_ref[slot, pl.ds(part * 16, 16), :]
                for a in range(8):
                    block = blocks(slot, row + a, part).astype(F32)
                    product = block * x
                    product = product[:8] + product[8:]
                    sums[a] = product if sums[a] is None else sums[a] + product
        index = iota((8, lanes), 0)
        total = jnp.zeros((8, lanes), F32)
        for a in range(8):
            total = jnp.where(index == a, jnp.sum(sums[a], axis=0, keepdims=True), total)
        place = pl.ds(pl.multiple_of(row, 8), 8)
        out_ref[place, :] = out_ref[place, :] + total if add else total


def kernel(
    weight,
    rhs_hbm,
    fine_hbm,
    columns_hbm,
    send_hbm,
    aggregate_hbm,
    coarse_hbm,
    ccolumns_hbm,
    smoother_hbm,
    out_ref,
    rhs_ref,
    columns_ref,
    send_ref,
    aggregate_ref,
    ccolumns_ref,
    fine,
    wide,
    coarse,
    smoother,
    coarse_raw,
    smoother_raw,
    x_ref,
    ax_ref,
    pivots_ref,
    state_ref,
    pick_own,
    pick_halo,
    pick_section,
    pick_coarse,
    send_onehot,
    halo_out,
    halo_in,
    part_out,
    part_in,
    first_all,
    z_out,
    z_in,
    half_out,
    half_in,
    cx_ref,
    cy_ref,
    load_sem,
    send_sems,
    recv_sems,
):
    s = lax.axis_index("sec")
    t = lax.axis_index("dev")
    sx, sz = s // N_Z, lax.rem(s, N_Z)
    chip, core = t // 2, lax.rem(t, 2)

    def dev_peer(p):
        return (s, (t + p) & (N_DEV - 1))

    def sec_peer(p):
        dx, dz = p // N_Z, p % N_Z
        z = sz + dz
        z = jnp.where(z >= N_Z, z - N_Z, z)
        return (((sx + dx) & (N_X - 1)) * N_Z + z, t)

    def chip_peer(p):
        return (s, (t + 2 * p) & (N_DEV - 1))

    other = (s, t + 1 - 2 * core)

    barrier = pltpu.get_barrier_semaphore()

    for p in SEC_ORDER:
        pl.semaphore_signal(barrier, inc=1, device_id=sec_peer(p), device_id_type=MESH)
    for p in DEV_ORDER:
        pl.semaphore_signal(barrier, inc=1, device_id=dev_peer(p), device_id_type=MESH)

    loads = [pltpu.make_async_copy(fine_hbm.at[k], fine.at[k], load_sem.at[k]) for k in range(4)]
    small = [
        pltpu.make_async_copy(*pair, load_sem.at[6 + n])
        for n, pair in enumerate(
            (
                (rhs_hbm, rhs_ref),
                (columns_hbm, columns_ref),
                (send_hbm, send_ref),
                (aggregate_hbm, aggregate_ref),
                (ccolumns_hbm, ccolumns_ref),
            )
        )
    ]
    for load in small:
        load.start()
    loads.append(pltpu.make_async_copy(smoother_hbm, smoother_raw, load_sem.at[4]))
    loads.append(
        pltpu.make_async_copy(coarse_hbm.at[:, pl.ds(core * 32, 32)], coarse_raw, load_sem.at[5])
    )
    for load in loads:
        load.start()
    for load in small:
        load.wait()

    aggregate = aggregate_ref[...]
    own_group = onehot_of(iota((COARSE, ROWS), 0) == aggregate)
    sent = jnp.concatenate(
        [send_ref[...], jnp.full((1, ROWS - 2 * HALO), -1, jnp.int32)], axis=1
    )
    sent = jnp.where(iota((ROWS, ROWS), 0) == sent, 1.0, 0.0).T
    send_onehot[...] = sent[: 2 * HALO].astype(BF16)
    row = iota((16, 4 * COARSE), 0)
    lane = iota((16, 4 * COARSE), 1)
    own_row = chip * 4 + jnp.where(lane < 2 * COARSE, row, row + 32)
    own_wide = onehot_of(((lane & (COARSE - 1)) == own_row) & (row < 4))
    row, lane = iota((16, 2 * COARSE), 0), iota((16, 2 * COARSE), 1)
    own_lane = ((row >> 2) & 1) * COARSE + (row >> 3) * 32 + chip * 4 + (row & 3)
    own_first = onehot_of(lane == own_lane)

    def fine_tables():
        for k in range(3):
            column = columns_ref[pl.ds(k, 1), :]
            pick_own[:, pl.ds(k * ROWS, ROWS)] = onehot_of(iota((ROWS, ROWS), 0) == column - HALO)
            slot = iota((2 * HALO, ROWS), 0)
            where = jnp.where(slot < HALO, slot, slot + ROWS)
            pick_halo[:, pl.ds(k * ROWS, ROWS)] = onehot_of(where == column)

    def coarse_tables():
        for k in range(4):
            column = ccolumns_ref[pl.ds(k, 1), :]
            section = column >> 6
            cx = (
                (section >= N_Z).astype(jnp.int32)
                + (section >= 2 * N_Z).astype(jnp.int32)
                + (section >= 3 * N_Z).astype(jnp.int32)
            )
            cz = section - cx * N_Z
            dx, dz = sx - cx, sz - cz
            dx = jnp.where(dx < 0, dx + N_X, dx)
            dz = jnp.where(dz < 0, dz + N_Z, dz)
            place = (dx * N_Z + dz) * 4 + (column & 3)
            place = jnp.where(((column & 31) >> 2) == chip, place, -1)
            for half in range(2):
                here = twice(jnp.where(((column >> 5) & 1) == half, place, -1))
                pick_coarse[:, pl.ds((4 * half + k) * 2 * COARSE, 2 * COARSE)] = onehot_of(
                    iota((N_SEC * 4, 2 * COARSE), 0) == here
                )

    loads[0].wait()
    index = iota((8, ROWS), 0)
    for tile in range(8):
        found = jnp.zeros((8, ROWS), F32)
        for a in range(8):
            i = tile * 8 + a
            near = fine[0, i, pl.ds(16 * (i // 16), 16), :].astype(F32)
            near = near[8 * (tile % 2) : 8 * (tile % 2) + 8]
            found = jnp.where(index == a, near, found)
        pivots_ref[pl.ds(tile * 8, 8), :] = found

    state_ref[...] = OMEGA * rhs_ref[...] / pivots_ref[...]

    def fine_block(slot, i, part):
        return fine[slot, i, pl.ds(part * 16, 16), :]

    def wide_block(slot, i, part):
        return wide[slot, i, pl.ds(part * 16, 16), :]

    def coarse_block(slot, i, part):
        return coarse[slot, i, pl.ds(part * 16, 16), :]

    def smoother_block(slot, i, part):
        return smoother[i, pl.ds(part * 16, 16), :]

    def wait_for(ref, sem):
        pltpu.make_async_copy(ref, ref, sem).wait()

    def halo_exchange(turn, with_groups):
        high, low = pieces(state_ref[...])
        picked = dot(send_onehot[...], high, NT) + dot(send_onehot[...], low, NT)
        if with_groups:
            groups = dot(send_onehot[...], own_group, NT)
        else:
            groups = jnp.zeros((2 * HALO, COARSE), F32)
        halo_out[turn] = jnp.concatenate([picked, groups], axis=1)
        if turn == 0:
            pl.semaphore_wait(barrier, N_DEV - 1 + N_SEC - 1)
        down = pltpu.make_async_remote_copy(
            src_ref=halo_out.at[turn, pl.ds(0, HALO)],
            dst_ref=halo_in.at[turn, pl.ds(HALO, HALO)],
            send_sem=send_sems.at[turn, 0],
            recv_sem=recv_sems.at[turn, 0],
            device_id=dev_peer(N_DEV - 1),
            device_id_type=MESH,
        )
        up = pltpu.make_async_remote_copy(
            src_ref=halo_out.at[turn, pl.ds(HALO, HALO)],
            dst_ref=halo_in.at[turn, pl.ds(0, HALO)],
            send_sem=send_sems.at[turn, 1],
            recv_sem=recv_sems.at[turn, 1],
            device_id=dev_peer(1),
            device_id_type=MESH,
        )
        down.start()
        up.start()
        x_ref[0] = state_ref[...]
        if turn == 0:
            fine_tables()
        blocks = fine_block if turn == 0 else wide_block
        multiply(blocks, (0,), 8, x_ref, ax_ref)
        own = dot(high, pick_own[...], NN) + dot(low, pick_own[...], NN)
        down.wait_recv()
        up.wait_recv()
        slot = iota((2 * HALO, ROWS), 0)
        there = ((slot < HALO) & (t > 0)) | ((slot >= HALO) & (t < N_DEV - 1))
        halo = jnp.where(there, halo_in[turn], 0.0)
        picked = own + select_right(halo[:, :BLOCK], pick_halo[...], TN)
        for k in range(3):
            x_ref[k + 1] = picked[:, k * ROWS : (k + 1) * ROWS]
        if with_groups:
            pick_section[:, pl.ds(0, ROWS)] = own_group
            pick_section[:, pl.ds(ROWS, 3 * ROWS)] = (
                dot(own_group, pick_own[...], NN)
                + dot(halo[:, BLOCK:].astype(BF16), pick_halo[...], TN)
            ).astype(BF16)
            for load in loads[1:4]:
                load.wait()
        multiply(blocks, (1, 2, 3), 8, x_ref, ax_ref, add=True)
        return down, up

    halo_copies = ()
    for cycle in range(CYCLES):
        base = 4 * cycle + 3
        if cycle > 0:
            halo_copies += halo_exchange(1, False)
            state_ref[...] += OMEGA * (rhs_ref[...] - ax_ref[...]) / pivots_ref[...]
        halo_copies += halo_exchange(2 * cycle, cycle == 0)
        residual = rhs_ref[...] - ax_ref[...]
        partial = select_left(own_group, residual, NT) * weight
        part_out[cycle] = jnp.concatenate([partial[:32], partial[32:]], axis=1).reshape(
            CHIPS, 4, 2 * BLOCK
        )

        for p in DEV_ORDER:
            pltpu.make_async_remote_copy(
                src_ref=part_out.at[cycle, ((t + p) & (N_DEV - 1)) >> 1],
                dst_ref=part_in.at[cycle, p - 1],
                send_sem=send_sems.at[base, 0],
                recv_sem=recv_sems.at[base, 0],
                device_id=dev_peer(p),
                device_id_type=MESH,
            ).start()

        if cycle == 0:
            loads[4].wait()

            @pl.loop(0, 32)
            def _(i):
                smoother[i] = jnp.concatenate([smoother_raw[i], smoother_raw[i + 32]], axis=1)

            coarse_tables()
        wait_for(part_in.at[cycle], recv_sems.at[base, 0])
        rhs_rows = part_out[cycle, chip] + jnp.sum(part_in[cycle], axis=0)
        rhs_rows = jnp.concatenate([rhs_rows, jnp.zeros((12, 2 * BLOCK), F32)], axis=0)
        wide_rhs = select_right(rhs_rows, own_wide, TN)
        cx_ref[0] = wide_rhs[:BLOCK, : 2 * COARSE] + wide_rhs[BLOCK:, 2 * COARSE :]
        multiply(smoother_block, (0,), 4, cx_ref, cy_ref)
        first = select_left(own_first, cy_ref[...], NT)
        first_all[cycle, 0] = jnp.concatenate([first[4 * n : 4 * n + 4] for n in range(4)], axis=1)

        for p in SEC_ORDER:
            pltpu.make_async_remote_copy(
                src_ref=first_all.at[cycle, 0],
                dst_ref=first_all.at[cycle, p],
                send_sem=send_sems.at[base + 1, 0],
                recv_sem=recv_sems.at[base + 1, 0],
                device_id=sec_peer(p),
                device_id_type=MESH,
            ).start()

        if cycle == 0:
            @pl.loop(0, BLOCK)
            def _(i):
                for k in range(4):
                    wide[k, i] = fine[k, i].astype(F32)

            loads[5].wait()

            @pl.loop(0, 16)
            def _(i):
                for k in range(5):
                    coarse[k, i] = jnp.concatenate([coarse_raw[k, i], coarse_raw[k, i + 16]], axis=1)

        coarse_rhs = cx_ref[0]
        cx_ref[0] = twice(unpaired(cy_ref[...]))
        multiply(coarse_block, (0,), 2, cx_ref, cy_ref)
        wait_for(first_all.at[cycle, pl.ds(1, N_SEC - 1)], recv_sems.at[base + 1, 0])
        held = first_all[cycle].reshape(N_SEC * 4, 2 * BLOCK)
        picked = select_right(held, pick_coarse[...], TN)
        picked = picked[:BLOCK, : 8 * COARSE] + picked[BLOCK:, 8 * COARSE :]
        for k in range(4):
            cx_ref[k + 1] = picked[:, k * 2 * COARSE : (k + 1) * 2 * COARSE]
        multiply(coarse_block, (1, 2, 3, 4), 2, cx_ref, cy_ref, add=True)
        own_half = jnp.where(core == 0, coarse_rhs[:32], coarse_rhs[32:])
        own_half = jnp.where(
            iota((16, 2 * COARSE), 1) < COARSE, own_half[:16], own_half[16:]
        )
        z_out[cycle] = 2.0 * own_half - cy_ref[pl.ds(0, 16), :]

        for p in CHIP_ORDER:
            pltpu.make_async_remote_copy(
                src_ref=z_out.at[cycle],
                dst_ref=z_in.at[cycle, p - 1],
                send_sem=send_sems.at[base + 2, 0],
                recv_sem=recv_sems.at[base + 2, 0],
                device_id=chip_peer(p),
                device_id_type=MESH,
            ).start()

        wait_for(z_in.at[cycle], recv_sems.at[base + 2, 0])
        half_out[cycle] = z_out[cycle] + jnp.sum(z_in[cycle], axis=0)
        pair = pltpu.make_async_remote_copy(
            src_ref=half_out.at[cycle],
            dst_ref=half_in.at[cycle],
            send_sem=send_sems.at[base + 3, 0],
            recv_sem=recv_sems.at[base + 3, 0],
            device_id=other,
            device_id_type=MESH,
        )
        pair.start()
        pair.wait_recv()
        mine, theirs = half_out[cycle], half_in[cycle]
        lower = jnp.where(core == 0, mine, theirs)
        upper = jnp.where(core == 0, theirs, mine)
        cx_ref[0] = twice(jnp.concatenate([unpaired(lower), unpaired(upper)], axis=0))
        multiply(smoother_block, (0,), 4, cx_ref, cy_ref)
        picked = select_right(unpaired(cy_ref[...]), pick_section[...], NN)
        for k in range(4):
            x_ref[k] = picked[:, k * ROWS : (k + 1) * ROWS]
        multiply(wide_block, (0, 1, 2, 3), 8, x_ref, ax_ref)
        state_ref[...] += PROLONG * x_ref[0] + OMEGA * (residual - PROLONG * ax_ref[...]) / (
            pivots_ref[...]
        )

        wait_for(part_in.at[cycle], send_sems.at[base, 0])
        wait_for(first_all.at[cycle, pl.ds(1, N_SEC - 1)], send_sems.at[base + 1, 0])
        wait_for(z_in.at[cycle], send_sems.at[base + 2, 0])
        pair.wait_send()

    out_ref[...] = state_ref[...]
    for copy in halo_copies:
        copy.wait_send()


def shards(
    right_side,
    fine_blocks,
    fine_columns,
    send_rows,
    aggregate,
    coarse_blocks,
    coarse_columns,
    coarse_smoother,
):
    vmem = pl.BlockSpec(memory_space=pltpu.VMEM)
    hbm = pl.BlockSpec(memory_space=pl.ANY)
    phases = 3 + 4 * CYCLES
    operands = [
        pltpu.with_memory_space_constraint(operand, pltpu.MemorySpace.HBM)
        for operand in (
            right_side,
            fine_blocks,
            fine_columns,
            send_rows.reshape(1, 2 * HALO),
            aggregate.reshape(1, ROWS),
            coarse_blocks,
            coarse_columns,
            coarse_smoother,
        )
    ]
    return pl.pallas_call(
        functools.partial(kernel, math.sqrt(4 / ROWS)),
        out_shape=jax.ShapeDtypeStruct((BLOCK, ROWS), F32),
        in_specs=[hbm] * 8,
        out_specs=vmem,
        scratch_shapes=[
            pltpu.VMEM((BLOCK, ROWS), F32),
            pltpu.VMEM((3, ROWS), jnp.int32),
            pltpu.VMEM((1, 2 * HALO), jnp.int32),
            pltpu.VMEM((1, ROWS), jnp.int32),
            pltpu.VMEM((4, COARSE), jnp.int32),
            pltpu.VMEM((4, BLOCK, BLOCK, ROWS), BF16),
            pltpu.VMEM((4, BLOCK, BLOCK, ROWS), F32),
            pltpu.VMEM((5, BLOCK // 4, BLOCK, 2 * COARSE), BF16),
            pltpu.VMEM((BLOCK // 2, BLOCK, 2 * COARSE), BF16),
            pltpu.VMEM((5, BLOCK // 2, BLOCK, COARSE), BF16),
            pltpu.VMEM((BLOCK, BLOCK, COARSE), BF16),
            pltpu.VMEM((4, BLOCK, ROWS), F32),
            pltpu.VMEM((BLOCK, ROWS), F32),
            pltpu.VMEM((BLOCK, ROWS), F32),
            pltpu.VMEM((BLOCK, ROWS), F32),
            pltpu.VMEM((ROWS, 3 * ROWS), BF16),
            pltpu.VMEM((2 * HALO, 3 * ROWS), BF16),
            pltpu.VMEM((COARSE, 4 * ROWS), BF16),
            pltpu.VMEM((N_SEC * 4, 16 * COARSE), BF16),
            pltpu.VMEM((2 * HALO, ROWS), BF16),
            pltpu.VMEM((3, 2 * HALO, 2 * BLOCK), F32),
            pltpu.VMEM((3, 2 * HALO, 2 * BLOCK), F32),
            pltpu.VMEM((CYCLES, CHIPS, 4, 2 * BLOCK), F32),
            pltpu.VMEM((CYCLES, N_DEV - 1, 4, 2 * BLOCK), F32),
            pltpu.VMEM((CYCLES, N_SEC, 4, 2 * BLOCK), F32),
            pltpu.VMEM((CYCLES, 16, 2 * COARSE), F32),
            pltpu.VMEM((CYCLES, CHIPS - 1, 16, 2 * COARSE), F32),
            pltpu.VMEM((CYCLES, 16, 2 * COARSE), F32),
            pltpu.VMEM((CYCLES, 16, 2 * COARSE), F32),
            pltpu.VMEM((5, BLOCK, 2 * COARSE), F32),
            pltpu.VMEM((BLOCK // 2, 2 * COARSE), F32),
            pltpu.SemaphoreType.DMA((11,)),
            pltpu.SemaphoreType.DMA((phases, 2)),
            pltpu.SemaphoreType.DMA((phases, 2)),
        ],
        compiler_params=pltpu.CompilerParams(
            collective_id=0, has_side_effects=True, vmem_limit_bytes=48 * 1024 * 1024
        ),
        name="cycles",
    )(*operands)


def solution(mesh):
    placed = (
        P(None, ("sec", "dev")),
        P(None, None, None, ("sec", "dev")),
        P(None, ("sec", "dev")),
        P(("sec", "dev")),
        P(("sec", "dev")),
        P(None, None, None, "sec"),
        P(None, "sec"),
        P(None, None, "sec"),
    )
    return jax.shard_map(
        shards, mesh=mesh, in_specs=placed, out_specs=P(None, ("sec", "dev")), check_vma=False
    )
```

```python
import functools
import math

import jax
import jax.numpy as jnp
from jax import lax
from jax.experimental import pallas as pl
from jax.experimental.pallas import tpu as pltpu
from jax.sharding import PartitionSpec as P

BLOCK = 64
ROWS = 128
HALO = 8
CYCLES = 2
N_DEV = 16
N_X = 4
N_Z = 12
N_SEC = N_X * N_Z
CHIPS = N_DEV // 2
COARSE = 64
OMEGA = 0.45
PROLONG = 0.5
MESH = pl.DeviceIdType.MESH
F32 = jnp.float32
BF16 = jnp.bfloat16
NT = (((1,), (1,)), ((), ()))
TN = (((0,), (0,)), ((), ()))
NN = (((1,), (0,)), ((), ()))


def ring(step, count):
    return min(step, count - step)


SEC_ORDER = sorted(
    range(1, N_SEC), key=lambda p: -(ring(p // N_Z, N_X) + ring(p % N_Z, N_Z))
)
DEV_ORDER = sorted(range(1, N_DEV), key=lambda p: -ring(p, N_DEV))


def pieces(value):
    high = value.astype(BF16)
    low = (value - high.astype(F32)).astype(BF16)
    return high, low


def dot(a, b, dims):
    return lax.dot_general(a, b, dims, preferred_element_type=F32)


def select_right(value, onehot, dims):
    high, low = pieces(value)
    return dot(high, onehot, dims) + dot(low, onehot, dims)


def select_left(onehot, value, dims):
    high, low = pieces(value)
    return dot(onehot, high, dims) + dot(onehot, low, dims)


def iota(shape, axis):
    return lax.broadcasted_iota(jnp.int32, shape, axis)


def onehot_of(condition):
    return jnp.where(condition, 1.0, 0.0).astype(BF16)


def twice(value):
    return jnp.concatenate([value, value], axis=1)


def unpaired(value):
    return jnp.concatenate([value[:, :COARSE], value[:, COARSE:]], axis=0)


def multiply(blocks, slots, tiles, x_ref, out_ref, add=False):
    lanes = x_ref.shape[-1]

    @pl.loop(0, tiles, unroll=2)
    def _(tile):
        row = tile * 8
        sums = [None] * 8
        for slot in slots:
            for part in range(BLOCK // 16):
                x = x_ref[slot, pl.ds(part * 16, 16), :]
                for a in range(8):
                    block = blocks(slot, row + a, part).astype(F32)
                    product = block * x
                    product = product[:8] + product[8:]
                    sums[a] = product if sums[a] is None else sums[a] + product
        index = iota((8, lanes), 0)
        total = jnp.zeros((8, lanes), F32)
        for a in range(8):
            total = jnp.where(index == a, jnp.sum(sums[a], axis=0, keepdims=True), total)
        place = pl.ds(pl.multiple_of(row, 8), 8)
        out_ref[place, :] = out_ref[place, :] + total if add else total


def kernel(
    weight,
    rhs_hbm,
    fine_hbm,
    columns_hbm,
    send_hbm,
    aggregate_hbm,
    coarse_hbm,
    ccolumns_hbm,
    smoother_hbm,
    out_ref,
    rhs_ref,
    columns_ref,
    send_ref,
    aggregate_ref,
    ccolumns_ref,
    fine,
    wide,
    coarse,
    smoother,
    coarse_raw,
    smoother_raw,
    x_ref,
    ax_ref,
    pivots_ref,
    state_ref,
    pick_own,
    pick_halo,
    pick_section,
    pick_coarse,
    send_onehot,
    halo_out,
    halo_in,
    part_out,
    part_in,
    first_all,
    z_out,
    z_in,
    cx_ref,
    cy_ref,
    load_sem,
    send_sems,
    recv_sems,
):
    s = lax.axis_index("sec")
    t = lax.axis_index("dev")
    sx, sz = s // N_Z, lax.rem(s, N_Z)
    chip, core = t // 2, lax.rem(t, 2)

    def dev_peer(p):
        return (s, (t + p) & (N_DEV - 1))

    def sec_peer(p):
        dx, dz = p // N_Z, p % N_Z
        z = sz + dz
        z = jnp.where(z >= N_Z, z - N_Z, z)
        return (((sx + dx) & (N_X - 1)) * N_Z + z, t)

    barrier = pltpu.get_barrier_semaphore()

    for p in SEC_ORDER:
        pl.semaphore_signal(barrier, inc=1, device_id=sec_peer(p), device_id_type=MESH)
    for p in DEV_ORDER:
        pl.semaphore_signal(barrier, inc=1, device_id=dev_peer(p), device_id_type=MESH)

    loads = [pltpu.make_async_copy(fine_hbm.at[k], fine.at[k], load_sem.at[k]) for k in range(4)]
    small = [
        pltpu.make_async_copy(*pair, load_sem.at[6 + n])
        for n, pair in enumerate(
            (
                (rhs_hbm, rhs_ref),
                (columns_hbm, columns_ref),
                (send_hbm, send_ref),
                (aggregate_hbm, aggregate_ref),
                (ccolumns_hbm, ccolumns_ref),
            )
        )
    ]
    for load in small:
        load.start()
    loads.append(pltpu.make_async_copy(smoother_hbm, smoother_raw, load_sem.at[4]))
    loads.append(
        pltpu.make_async_copy(coarse_hbm.at[:, pl.ds(core * 32, 32)], coarse_raw, load_sem.at[5])
    )
    for load in loads:
        load.start()
    for load in small:
        load.wait()

    aggregate = aggregate_ref[...]
    own_group = onehot_of(iota((COARSE, ROWS), 0) == aggregate)
    sent = jnp.concatenate(
        [send_ref[...], jnp.full((1, ROWS - 2 * HALO), -1, jnp.int32)], axis=1
    )
    sent = jnp.where(iota((ROWS, ROWS), 0) == sent, 1.0, 0.0).T
    send_onehot[...] = sent[: 2 * HALO].astype(BF16)
    row = iota((16, 4 * COARSE), 0)
    lane = iota((16, 4 * COARSE), 1)
    own_row = chip * 4 + jnp.where(lane < 2 * COARSE, row, row + 32)
    own_wide = onehot_of(((lane & (COARSE - 1)) == own_row) & (row < 4))
    row, lane = iota((16, 2 * COARSE), 0), iota((16, 2 * COARSE), 1)
    own_lane = ((row >> 2) & 1) * COARSE + (row >> 3) * 32 + chip * 4 + (row & 3)
    own_first = onehot_of(lane == own_lane)

    def fine_tables():
        for k in range(3):
            column = columns_ref[pl.ds(k, 1), :]
            pick_own[:, pl.ds(k * ROWS, ROWS)] = onehot_of(iota((ROWS, ROWS), 0) == column - HALO)
            slot = iota((2 * HALO, ROWS), 0)
            where = jnp.where(slot < HALO, slot, slot + ROWS)
            pick_halo[:, pl.ds(k * ROWS, ROWS)] = onehot_of(where == column)

    def coarse_tables():
        for k in range(4):
            column = ccolumns_ref[pl.ds(k, 1), :]
            section = column >> 6
            cx = (
                (section >= N_Z).astype(jnp.int32)
                + (section >= 2 * N_Z).astype(jnp.int32)
                + (section >= 3 * N_Z).astype(jnp.int32)
            )
            cz = section - cx * N_Z
            dx, dz = sx - cx, sz - cz
            dx = jnp.where(dx < 0, dx + N_X, dx)
            dz = jnp.where(dz < 0, dz + N_Z, dz)
            place = (dx * N_Z + dz) * 4 + (column & 3)
            place = jnp.where(((column & 31) >> 2) == chip, place, -1)
            for half in range(2):
                here = twice(jnp.where(((column >> 5) & 1) == half, place, -1))
                pick_coarse[:, pl.ds((4 * half + k) * 2 * COARSE, 2 * COARSE)] = onehot_of(
                    iota((N_SEC * 4, 2 * COARSE), 0) == here
                )

    loads[0].wait()
    index = iota((8, ROWS), 0)
    for tile in range(8):
        found = jnp.zeros((8, ROWS), F32)
        for a in range(8):
            i = tile * 8 + a
            near = fine[0, i, pl.ds(16 * (i // 16), 16), :].astype(F32)
            near = near[8 * (tile % 2) : 8 * (tile % 2) + 8]
            found = jnp.where(index == a, near, found)
        pivots_ref[pl.ds(tile * 8, 8), :] = found

    state_ref[...] = OMEGA * rhs_ref[...] / pivots_ref[...]

    def fine_block(slot, i, part):
        return fine[slot, i, pl.ds(part * 16, 16), :]

    def wide_block(slot, i, part):
        return wide[slot, i, pl.ds(part * 16, 16), :]

    def coarse_block(slot, i, part):
        return coarse[slot, i, pl.ds(part * 16, 16), :]

    def smoother_block(slot, i, part):
        return smoother[i, pl.ds(part * 16, 16), :]

    def wait_for(ref, sem):
        pltpu.make_async_copy(ref, ref, sem).wait()

    def halo_exchange(turn, with_groups):
        high, low = pieces(state_ref[...])
        picked = dot(send_onehot[...], high, NT) + dot(send_onehot[...], low, NT)
        if with_groups:
            groups = dot(send_onehot[...], own_group, NT)
        else:
            groups = jnp.zeros((2 * HALO, COARSE), F32)
        halo_out[turn] = jnp.concatenate([picked, groups], axis=1)
        if turn == 0:
            pl.semaphore_wait(barrier, N_DEV - 1 + N_SEC - 1)
        down = pltpu.make_async_remote_copy(
            src_ref=halo_out.at[turn, pl.ds(0, HALO)],
            dst_ref=halo_in.at[turn, pl.ds(HALO, HALO)],
            send_sem=send_sems.at[turn, 0],
            recv_sem=recv_sems.at[turn, 0],
            device_id=dev_peer(N_DEV - 1),
            device_id_type=MESH,
        )
        up = pltpu.make_async_remote_copy(
            src_ref=halo_out.at[turn, pl.ds(HALO, HALO)],
            dst_ref=halo_in.at[turn, pl.ds(0, HALO)],
            send_sem=send_sems.at[turn, 1],
            recv_sem=recv_sems.at[turn, 1],
            device_id=dev_peer(1),
            device_id_type=MESH,
        )
        down.start()
        up.start()
        x_ref[0] = state_ref[...]
        if turn == 0:
            fine_tables()
        blocks = fine_block if turn == 0 else wide_block
        multiply(blocks, (0,), 8, x_ref, ax_ref)
        own = dot(high, pick_own[...], NN) + dot(low, pick_own[...], NN)
        down.wait_recv()
        up.wait_recv()
        slot = iota((2 * HALO, ROWS), 0)
        there = ((slot < HALO) & (t > 0)) | ((slot >= HALO) & (t < N_DEV - 1))
        halo = jnp.where(there, halo_in[turn], 0.0)
        picked = own + select_right(halo[:, :BLOCK], pick_halo[...], TN)
        for k in range(3):
            x_ref[k + 1] = picked[:, k * ROWS : (k + 1) * ROWS]
        if with_groups:
            pick_section[:, pl.ds(0, ROWS)] = own_group
            pick_section[:, pl.ds(ROWS, 3 * ROWS)] = (
                dot(own_group, pick_own[...], NN)
                + dot(halo[:, BLOCK:].astype(BF16), pick_halo[...], TN)
            ).astype(BF16)
            for load in loads[1:4]:
                load.wait()
        multiply(blocks, (1, 2, 3), 8, x_ref, ax_ref, add=True)
        return down, up

    halo_copies = ()
    for cycle in range(CYCLES):
        base = 4 * cycle + 3
        if cycle > 0:
            halo_copies += halo_exchange(1, False)
            state_ref[...] += OMEGA * (rhs_ref[...] - ax_ref[...]) / pivots_ref[...]
        halo_copies += halo_exchange(2 * cycle, cycle == 0)
        residual = rhs_ref[...] - ax_ref[...]
        partial = select_left(own_group, residual, NT) * weight
        part_out[cycle] = jnp.concatenate([partial[:32], partial[32:]], axis=1).reshape(
            CHIPS, 4, 2 * BLOCK
        )

        for p in DEV_ORDER:
            pltpu.make_async_remote_copy(
                src_ref=part_out.at[cycle, ((t + p) & (N_DEV - 1)) >> 1],
                dst_ref=part_in.at[cycle, p - 1],
                send_sem=send_sems.at[base, 0],
                recv_sem=recv_sems.at[base, 0],
                device_id=dev_peer(p),
                device_id_type=MESH,
            ).start()

        if cycle == 0:
            loads[4].wait()

            @pl.loop(0, 32)
            def _(i):
                smoother[i] = jnp.concatenate([smoother_raw[i], smoother_raw[i + 32]], axis=1)

            coarse_tables()
        wait_for(part_in.at[cycle], recv_sems.at[base, 0])
        rhs_rows = part_out[cycle, chip] + jnp.sum(part_in[cycle], axis=0)
        rhs_rows = jnp.concatenate([rhs_rows, jnp.zeros((12, 2 * BLOCK), F32)], axis=0)
        wide_rhs = select_right(rhs_rows, own_wide, TN)
        cx_ref[0] = wide_rhs[:BLOCK, : 2 * COARSE] + wide_rhs[BLOCK:, 2 * COARSE :]
        multiply(smoother_block, (0,), 4, cx_ref, cy_ref)
        first = select_left(own_first, cy_ref[...], NT)
        first_all[cycle, 0] = jnp.concatenate([first[4 * n : 4 * n + 4] for n in range(4)], axis=1)

        for p in SEC_ORDER:
            pltpu.make_async_remote_copy(
                src_ref=first_all.at[cycle, 0],
                dst_ref=first_all.at[cycle, p],
                send_sem=send_sems.at[base + 1, 0],
                recv_sem=recv_sems.at[base + 1, 0],
                device_id=sec_peer(p),
                device_id_type=MESH,
            ).start()

        if cycle == 0:
            @pl.loop(0, BLOCK)
            def _(i):
                for k in range(4):
                    wide[k, i] = fine[k, i].astype(F32)

            loads[5].wait()

            @pl.loop(0, 16)
            def _(i):
                for k in range(5):
                    coarse[k, i] = jnp.concatenate([coarse_raw[k, i], coarse_raw[k, i + 16]], axis=1)

        coarse_rhs = cx_ref[0]
        cx_ref[0] = twice(unpaired(cy_ref[...]))
        multiply(coarse_block, (0,), 2, cx_ref, cy_ref)
        wait_for(first_all.at[cycle, pl.ds(1, N_SEC - 1)], recv_sems.at[base + 1, 0])
        held = first_all[cycle].reshape(N_SEC * 4, 2 * BLOCK)
        picked = select_right(held, pick_coarse[...], TN)
        picked = picked[:BLOCK, : 8 * COARSE] + picked[BLOCK:, 8 * COARSE :]
        for k in range(4):
            cx_ref[k + 1] = picked[:, k * 2 * COARSE : (k + 1) * 2 * COARSE]
        multiply(coarse_block, (1, 2, 3, 4), 2, cx_ref, cy_ref, add=True)
        own_half = jnp.where(core == 0, coarse_rhs[:32], coarse_rhs[32:])
        own_half = jnp.where(
            iota((16, 2 * COARSE), 1) < COARSE, own_half[:16], own_half[16:]
        )
        z_out[cycle] = 2.0 * own_half - cy_ref[pl.ds(0, 16), :]

        for p in DEV_ORDER:
            pltpu.make_async_remote_copy(
                src_ref=z_out.at[cycle],
                dst_ref=z_in.at[cycle, p - 1],
                send_sem=send_sems.at[base + 2, 0],
                recv_sem=recv_sems.at[base + 2, 0],
                device_id=dev_peer(p),
                device_id_type=MESH,
            ).start()

        wait_for(z_in.at[cycle], recv_sems.at[base + 2, 0])
        came = [z_in[cycle, p - 1] for p in range(1, N_DEV)]
        mine, theirs = z_out[cycle] + sum(came[1::2]), sum(came[0::2])
        lower = jnp.where(core == 0, mine, theirs)
        upper = jnp.where(core == 0, theirs, mine)
        cx_ref[0] = twice(jnp.concatenate([unpaired(lower), unpaired(upper)], axis=0))
        multiply(smoother_block, (0,), 4, cx_ref, cy_ref)
        picked = select_right(unpaired(cy_ref[...]), pick_section[...], NN)
        for k in range(4):
            x_ref[k] = picked[:, k * ROWS : (k + 1) * ROWS]
        multiply(wide_block, (0, 1, 2, 3), 8, x_ref, ax_ref)
        state_ref[...] += PROLONG * x_ref[0] + OMEGA * (residual - PROLONG * ax_ref[...]) / (
            pivots_ref[...]
        )

        wait_for(part_in.at[cycle], send_sems.at[base, 0])
        wait_for(first_all.at[cycle, pl.ds(1, N_SEC - 1)], send_sems.at[base + 1, 0])
        wait_for(z_in.at[cycle], send_sems.at[base + 2, 0])

    out_ref[...] = state_ref[...]
    for copy in halo_copies:
        copy.wait_send()


def shards(
    right_side,
    fine_blocks,
    fine_columns,
    send_rows,
    aggregate,
    coarse_blocks,
    coarse_columns,
    coarse_smoother,
):
    vmem = pl.BlockSpec(memory_space=pltpu.VMEM)
    hbm = pl.BlockSpec(memory_space=pl.ANY)
    phases = 3 + 4 * CYCLES
    operands = [
        pltpu.with_memory_space_constraint(operand, pltpu.MemorySpace.HBM)
        for operand in (
            right_side,
            fine_blocks,
            fine_columns,
            send_rows.reshape(1, 2 * HALO),
            aggregate.reshape(1, ROWS),
            coarse_blocks,
            coarse_columns,
            coarse_smoother,
        )
    ]
    return pl.pallas_call(
        functools.partial(kernel, math.sqrt(4 / ROWS)),
        out_shape=jax.ShapeDtypeStruct((BLOCK, ROWS), F32),
        in_specs=[hbm] * 8,
        out_specs=vmem,
        scratch_shapes=[
            pltpu.VMEM((BLOCK, ROWS), F32),
            pltpu.VMEM((3, ROWS), jnp.int32),
            pltpu.VMEM((1, 2 * HALO), jnp.int32),
            pltpu.VMEM((1, ROWS), jnp.int32),
            pltpu.VMEM((4, COARSE), jnp.int32),
            pltpu.VMEM((4, BLOCK, BLOCK, ROWS), BF16),
            pltpu.VMEM((4, BLOCK, BLOCK, ROWS), F32),
            pltpu.VMEM((5, BLOCK // 4, BLOCK, 2 * COARSE), BF16),
            pltpu.VMEM((BLOCK // 2, BLOCK, 2 * COARSE), BF16),
            pltpu.VMEM((5, BLOCK // 2, BLOCK, COARSE), BF16),
            pltpu.VMEM((BLOCK, BLOCK, COARSE), BF16),
            pltpu.VMEM((4, BLOCK, ROWS), F32),
            pltpu.VMEM((BLOCK, ROWS), F32),
            pltpu.VMEM((BLOCK, ROWS), F32),
            pltpu.VMEM((BLOCK, ROWS), F32),
            pltpu.VMEM((ROWS, 3 * ROWS), BF16),
            pltpu.VMEM((2 * HALO, 3 * ROWS), BF16),
            pltpu.VMEM((COARSE, 4 * ROWS), BF16),
            pltpu.VMEM((N_SEC * 4, 16 * COARSE), BF16),
            pltpu.VMEM((2 * HALO, ROWS), BF16),
            pltpu.VMEM((3, 2 * HALO, 2 * BLOCK), F32),
            pltpu.VMEM((3, 2 * HALO, 2 * BLOCK), F32),
            pltpu.VMEM((CYCLES, CHIPS, 4, 2 * BLOCK), F32),
            pltpu.VMEM((CYCLES, N_DEV - 1, 4, 2 * BLOCK), F32),
            pltpu.VMEM((CYCLES, N_SEC, 4, 2 * BLOCK), F32),
            pltpu.VMEM((CYCLES, 16, 2 * COARSE), F32),
            pltpu.VMEM((CYCLES, N_DEV - 1, 16, 2 * COARSE), F32),
            pltpu.VMEM((5, BLOCK, 2 * COARSE), F32),
            pltpu.VMEM((BLOCK // 2, 2 * COARSE), F32),
            pltpu.SemaphoreType.DMA((11,)),
            pltpu.SemaphoreType.DMA((phases, 2)),
            pltpu.SemaphoreType.DMA((phases, 2)),
        ],
        compiler_params=pltpu.CompilerParams(
            collective_id=0, has_side_effects=True, vmem_limit_bytes=48 * 1024 * 1024
        ),
        name="cycles",
    )(*operands)


def solution(mesh):
    placed = (
        P(None, ("sec", "dev")),
        P(None, None, None, ("sec", "dev")),
        P(None, ("sec", "dev")),
        P(("sec", "dev")),
        P(("sec", "dev")),
        P(None, None, None, "sec"),
        P(None, "sec"),
        P(None, None, "sec"),
    )
    return jax.shard_map(
        shards, mesh=mesh, in_specs=placed, out_specs=P(None, ("sec", "dev")), check_vma=False
    )
```
